32 devices in a mesh: seq: 4 (over x, core), row: 4 (over z), col: 2 (over y).
Axes of the slice: x: 2, y: 2, z: 4, core: 2. Of those that a mesh axis runs over, the one named last changes fastest.
Arguments:
- homolog_activations: bfloat16 [32, 64, 64], P(('seq', 'col'), 'row'), may hold values from -6 to 6
- alignment_token_ids: int32 [32, 64], P(('seq', 'col'), 'row'), may hold values from 0 to 79
- symbol_lookup_matrix: bfloat16 [80, 64], replicated, may hold values from -6 to 6
- homolog_rescale_vector: float32 [64], replicated, may hold values from 0.1 to 1.9
- first_operand_projection: bfloat16 [64, 32], replicated, may hold values from -0.75 to 0.75
- second_operand_projection: bfloat16 [64, 32], replicated, may hold values from -0.75 to 0.75
- outer_output_weight: bfloat16 [1024, 128], replicated, may hold values from -0.75 to 0.75
- outer_bias: float32 [128], replicated, may hold values from -3 to 3
- pair: bfloat16 [64, 64, 128], P('row', ('seq', 'col')), may hold values from -6 to 6
- pair_norm_gain: float32 [128], replicated, may hold values from 0.1 to 1.9
- pair_query_weight: bfloat16 [128, 128], replicated, as said below
- pair_key_weight: bfloat16 [128, 128], replicated, as said below
- pair_value_weight: bfloat16 [128, 128], replicated, may hold values from -0.5 to 0.5
- pair_gate_weight: bfloat16 [128, 128], replicated, may hold values from -0.5 to 0.5
- pair_output_weight: bfloat16 [128, 128], replicated, may hold values from -0.5 to 0.5
- nodes: bfloat16 [64, 64], P(('seq', 'col')), may hold values from -6 to 6
- coords: float32 [3, 64], P(None, ('seq', 'col')), may hold values from -18 to 18
- neighbour_index: int32 [64, 64], P(('seq', 'col')), may hold values from 0 to 63
- neighbour_count: int32 [64], P(('seq', 'col')), may hold values from 1 to 64, 2560 in all
- node_norm_gain: float32 [64], replicated, may hold values from 0.1 to 1.9
- node_query_weight: bfloat16 [64, 64], replicated, as said below
- node_key_weight: bfloat16 [64, 64], replicated, as said below
- node_value_weight: bfloat16 [64, 64], replicated, may hold values from -0.75 to 0.75
- node_output_weight: bfloat16 [64, 64], replicated, may hold values from -0.75 to 0.75
- distance_penalty: float32 [4], replicated, may hold values from 0.02 to 0.5
- coordinate_step: float32 [4], replicated, may hold values from -0.5 to 0.5
Outputs:
- pair_out: bfloat16 [64, 64, 128], P('row', ('seq', 'col'))
- nodes_out: bfloat16 [64, 64], P(('seq', 'col'))
- coords_out: float32 [3, 64], P(None, ('seq', 'col'))
The draws below stay inside these ranges and needn't reach their ends.
Inputs may be any that keep to these rules, and one draw needn't show every extreme that they name: `neighbour_index`: indices of residues; only the first neighbour_count[i] entries of row i are used. `pair_query_weight`: a projection matrix. `pair_key_weight`: a projection matrix. `node_query_weight`: a projection matrix. `node_key_weight`: a projection matrix.
All inputs are finite; a program needn't handle non-finite values. No bound on the sum of `neighbour_count` on one device may be relied on, other than what follows from the above.
Results may differ from the reference program's by a relative error of at most 0.02.
Values may be sent and summed in bfloat16 or wider, within the bound.
A program may use at most 64 MiB of HBM per device.

```python
import math
from functools import partial
import jax
import jax.numpy as jnp
import numpy as np
from jax import lax

HOMOLOG_TOTAL = 32
CHAIN_LENGTH = 64
ROW_FEATURE_DIM = 64
AMINO_VOCABULARY = 80
PRODUCT_WIDTH = 32
C_PAIR = 128
PAIR_HEADS = 4
C_NODE = 64
NODE_HEADS = 4
K = 64


def draw_pair_query_weight(key, part):
    key = jax.random.fold_in(key, 11)
    return (jax.random.normal(key, (C_PAIR, C_PAIR), jnp.float32) * C_PAIR ** (-0.5)).astype(jnp.bfloat16)


def draw_pair_key_weight(key, part):
    key = jax.random.fold_in(key, 12)
    return (jax.random.normal(key, (C_PAIR, C_PAIR), jnp.float32) * C_PAIR ** (-0.5)).astype(jnp.bfloat16)


def draw_node_query_weight(key, part):
    key = jax.random.fold_in(key, 13)
    return (jax.random.normal(key, (C_NODE, C_NODE), jnp.float32) * C_NODE ** (-0.5)).astype(jnp.bfloat16)


def draw_node_key_weight(key, part):
    key = jax.random.fold_in(key, 14)
    return (jax.random.normal(key, (C_NODE, C_NODE), jnp.float32) * C_NODE ** (-0.5)).astype(jnp.bfloat16)


def plant(entries, own_key, low, high):
    longest = entries.shape.index(max(entries.shape))
    spots = []
    for shift in (0, 1):
        where = [jax.random.randint(jax.random.fold_in(own_key, axis), (), 0, length) for axis, length in enumerate(entries.shape)]
        where[longest] = (where[longest] + shift) % entries.shape[longest]
        spots.append(tuple(where))
    return entries.at[spots[0]].set(low).at[spots[1]].set(high)


def block_scale(stream_key, dims, split, least, largest):
    def one(dim, blocks):
        heights = jax.random.uniform(jax.random.fold_in(jax.random.fold_in(stream_key, 6), dim), (blocks,), jnp.float32, least / len(split), largest / len(split))
        return jnp.repeat(jnp.exp(heights), dims[dim] // blocks).reshape((-1,) + (1,) * (len(dims) - dim - 1))

    gain = one(*split[0])
    for cut in split[1:]:
        gain = gain * one(*cut)
    return gain


def split_up(number_of, total, most, lean):
    loads = [(1 << 20) // math.isqrt(grade ** lean) + 1 for grade in range(2, number_of + 1)]
    surplus, counts = total - most - (number_of - 1), [1] * (number_of - 1)
    while surplus > 0:
        free = [i for i in range(number_of - 1) if counts[i] < most]
        mass, remaining = sum([loads[i] for i in free]), surplus
        for i in free:
            extra = min(most - counts[i], max(1, remaining * loads[i] // mass), surplus)
            counts[i] = counts[i] + extra
            surplus = surplus - extra
    return np.array([most] + counts)


def ragged(key, number_of, total, most, skew):
    if number_of == 2:
        one = jax.random.randint(key, (), max(1, total - most), min(most, total - 1) + 1)
        return jnp.stack([one, total - one])
    sizes = jnp.asarray(split_up(number_of, total, most, skew), jnp.int32)
    pairs = (number_of - 1) // 2
    source_of, taker = sizes[1:1 + 2 * pairs:2], sizes[2:2 + 2 * pairs:2]
    slack = jnp.minimum(source_of - 1, most - taker)
    shifted = jax.random.randint(jax.random.fold_in(key, 1), (pairs,), 0, 1 << 20) % (slack + 1)
    sizes = sizes.at[1:1 + 2 * pairs:2].set(source_of - shifted).at[2:2 + 2 * pairs:2].set(taker + shifted)
    return sizes[jax.random.permutation(jax.random.fold_in(key, 2), number_of)]


def scatter_about(own_key, dims, deviation, bound, split=(), kind=jnp.bfloat16):
    drawn = deviation * jax.random.normal(own_key, dims, jnp.float32)
    if split:
        drawn = drawn * block_scale(own_key, dims, split, -0.22, 0.18)
    return jnp.clip(drawn, -bound, bound).astype(kind)


def setup_inputs(seed: int = 0) -> dict:
    arg_keys = jax.random.split(jax.random.key(seed), 27)
    homolog_activations = scatter_about(arg_keys[0], (HOMOLOG_TOTAL, CHAIN_LENGTH, ROW_FEATURE_DIM), 1.0, 6.0, ((0, 8), (1, 4)))
    alignment_token_ids = plant(jax.random.randint(arg_keys[1], (HOMOLOG_TOTAL, CHAIN_LENGTH), 0, AMINO_VOCABULARY), jax.random.fold_in(arg_keys[1], 1), 0, AMINO_VOCABULARY - 1).astype(jnp.int32)
    symbol_lookup_matrix = scatter_about(arg_keys[2], (AMINO_VOCABULARY, ROW_FEATURE_DIM), 1.0, 6.0)
    homolog_rescale_vector = jnp.clip(1.0 + 0.18 * jax.random.normal(arg_keys[3], (ROW_FEATURE_DIM,), jnp.float32), 0.1, 1.9)
    first_operand_projection = scatter_about(arg_keys[4], (ROW_FEATURE_DIM, PRODUCT_WIDTH), ROW_FEATURE_DIM ** -0.5, 0.75)
    second_operand_projection = scatter_about(arg_keys[5], (ROW_FEATURE_DIM, PRODUCT_WIDTH), ROW_FEATURE_DIM ** -0.5, 0.75)
    outer_output_weight = scatter_about(arg_keys[6], (PRODUCT_WIDTH * PRODUCT_WIDTH, C_PAIR), (2 * PRODUCT_WIDTH) ** -0.5, 0.75)
    outer_bias = scatter_about(arg_keys[7], (C_PAIR,), 0.5, 3.0, (), jnp.float32)
    pair = scatter_about(arg_keys[8], (CHAIN_LENGTH, CHAIN_LENGTH, C_PAIR), 1.0, 6.0, ((0, 4), (1, 8)))
    pair_norm_gain = jnp.clip(1.0 + 0.18 * jax.random.normal(arg_keys[9], (C_PAIR,), jnp.float32), 0.1, 1.9)
    pair_query_weight = draw_pair_query_weight(jax.random.fold_in(arg_keys[26], 71), 0)
    pair_key_weight = draw_pair_key_weight(jax.random.fold_in(arg_keys[26], 71), 0)
    pair_value_weight = scatter_about(arg_keys[12], (C_PAIR, C_PAIR), C_PAIR ** -0.5, 0.5)
    pair_gate_weight = scatter_about(arg_keys[13], (C_PAIR, C_PAIR), C_PAIR ** -0.5, 0.5)
    pair_output_weight = scatter_about(arg_keys[14], (C_PAIR, C_PAIR), C_PAIR ** -0.5, 0.5)
    nodes = scatter_about(arg_keys[15], (CHAIN_LENGTH, C_NODE), 1.0, 6.0, ((0, 8),))
    coords = scatter_about(arg_keys[16], (3, CHAIN_LENGTH), 3.0, 18.0, ((1, 8),), jnp.float32)
    neighbour_index = plant(jax.random.randint(arg_keys[17], (CHAIN_LENGTH, K), 0, CHAIN_LENGTH), jax.random.fold_in(arg_keys[17], 1), 0, CHAIN_LENGTH - 1).astype(jnp.int32)
    neighbour_count = ragged(arg_keys[18], CHAIN_LENGTH, CHAIN_LENGTH * K * 5 // 8, K, 2).astype(jnp.int32)
    node_norm_gain = jnp.clip(1.0 + 0.18 * jax.random.normal(arg_keys[19], (C_NODE,), jnp.float32), 0.1, 1.9)
    node_query_weight = draw_node_query_weight(jax.random.fold_in(arg_keys[26], 71), 0)
    node_key_weight = draw_node_key_weight(jax.random.fold_in(arg_keys[26], 71), 0)
    node_value_weight = scatter_about(arg_keys[22], (C_NODE, C_NODE), C_NODE ** -0.5, 0.75)
    node_output_weight = scatter_about(arg_keys[23], (C_NODE, C_NODE), C_NODE ** -0.5, 0.75)
    distance_penalty = jnp.clip(jnp.exp(jax.random.uniform(arg_keys[24], (NODE_HEADS,), jnp.float32, math.log(0.02), math.log(0.5))), 0.02, 0.5)
    coordinate_step = jnp.clip(jax.random.uniform(arg_keys[25], (NODE_HEADS,), jnp.float32, -0.5, 0.5), -0.5, 0.5)
    return {"homolog_activations": homolog_activations, "alignment_token_ids": alignment_token_ids, "symbol_lookup_matrix": symbol_lookup_matrix, "homolog_rescale_vector": homolog_rescale_vector, "first_operand_projection": first_operand_projection, "second_operand_projection": second_operand_projection, "outer_output_weight": outer_output_weight, "outer_bias": outer_bias, "pair": pair, "pair_norm_gain": pair_norm_gain, "pair_query_weight": pair_query_weight, "pair_key_weight": pair_key_weight, "pair_value_weight": pair_value_weight, "pair_gate_weight": pair_gate_weight, "pair_output_weight": pair_output_weight, "nodes": nodes, "coords": coords, "neighbour_index": neighbour_index, "neighbour_count": neighbour_count, "node_norm_gain": node_norm_gain, "node_query_weight": node_query_weight, "node_key_weight": node_key_weight, "node_value_weight": node_value_weight, "node_output_weight": node_output_weight, "distance_penalty": distance_penalty, "coordinate_step": coordinate_step}


def layer_normalize(values_in, gain_vec):
    average = lax.optimization_barrier(jnp.mean(values_in, -1, keepdims=True))
    centred = values_in - average
    variance = lax.optimization_barrier(jnp.mean(centred * centred, -1, keepdims=True))
    return centred * lax.rsqrt(variance + 1e-05) * gain_vec.astype(jnp.float32)

def attend_row(row_in, gain_vec, w_query, w_key, w_value, w_gate, w_out):
    length, channels = row_in.shape
    head_dim = channels // PAIR_HEADS
    normed = layer_normalize(row_in.astype(jnp.float32), gain_vec).astype(jnp.bfloat16)
    queries = jnp.dot(normed, w_query, preferred_element_type=jnp.float32).astype(jnp.bfloat16)
    keys_row = jnp.dot(normed, w_key, preferred_element_type=jnp.float32).astype(jnp.bfloat16)
    values_row = jnp.dot(normed, w_value, preferred_element_type=jnp.float32).astype(jnp.bfloat16)
    gates = jnp.dot(normed, w_gate, preferred_element_type=jnp.float32)
    queries = queries.reshape(length, PAIR_HEADS, head_dim).astype(jnp.float32)
    keys_row = keys_row.reshape(length, PAIR_HEADS, head_dim).astype(jnp.float32)
    values_row = values_row.reshape(length, PAIR_HEADS, head_dim).astype(jnp.float32)
    scores = jnp.einsum('qhd,khd->hqk', queries, keys_row) * head_dim ** (-0.5)
    weights = jax.nn.softmax(scores, axis=-1).astype(jnp.bfloat16)
    attended = jnp.einsum('hqk,khd->qhd', weights.astype(jnp.float32), values_row).reshape(length, channels)
    attended = (attended * jax.nn.sigmoid(gates)).astype(jnp.bfloat16)
    update = jnp.dot(attended, w_out, preferred_element_type=jnp.float32)
    return (row_in.astype(jnp.float32) + update).astype(jnp.bfloat16)

def reference(homolog_activations, alignment_token_ids, symbol_lookup_matrix, homolog_rescale_vector, first_operand_projection, second_operand_projection, outer_output_weight, outer_bias, pair, pair_norm_gain, pair_query_weight, pair_key_weight, pair_value_weight, pair_gate_weight, pair_output_weight, nodes, coords, neighbour_index, neighbour_count, node_norm_gain, node_query_weight, node_key_weight, node_value_weight, node_output_weight, distance_penalty, coordinate_step):
    alignment_input = homolog_activations.astype(jnp.float32) + symbol_lookup_matrix[alignment_token_ids].astype(jnp.float32)
    alignment_normed = layer_normalize(alignment_input, homolog_rescale_vector)
    left_factor = jnp.dot(alignment_normed, first_operand_projection, preferred_element_type=jnp.float32).astype(jnp.bfloat16)
    right_factor = jnp.dot(alignment_normed, second_operand_projection, preferred_element_type=jnp.float32).astype(jnp.bfloat16)
    block_rows = 16

    def outer_block(first_row):
        left_rows = lax.dynamic_slice_in_dim(left_factor, first_row, block_rows, 1).astype(jnp.float32)
        summed = jnp.einsum('sic,sjd->ijcd', left_rows, right_factor.astype(jnp.float32))
        outer = (summed / HOMOLOG_TOTAL).reshape(block_rows, CHAIN_LENGTH, PRODUCT_WIDTH * PRODUCT_WIDTH).astype(jnp.bfloat16)
        update = jnp.dot(outer, outer_output_weight, preferred_element_type=jnp.float32) + outer_bias
        pair_rows = lax.dynamic_slice_in_dim(pair, first_row, block_rows, 0).astype(jnp.float32)
        return (pair_rows + update).astype(jnp.bfloat16)
    starts = (jnp.arange(CHAIN_LENGTH // block_rows) * block_rows).astype(jnp.int32)
    pair_mid = lax.map(outer_block, starts).reshape(CHAIN_LENGTH, CHAIN_LENGTH, C_PAIR)
    pair_out = lax.map(partial(attend_row, gain_vec=pair_norm_gain, w_query=pair_query_weight, w_key=pair_key_weight, w_value=pair_value_weight, w_gate=pair_gate_weight, w_out=pair_output_weight), pair_mid)
    node_dim = C_NODE // NODE_HEADS
    node_norm = layer_normalize(nodes.astype(jnp.float32), node_norm_gain).astype(jnp.bfloat16)
    node_query = jnp.dot(node_norm, node_query_weight, preferred_element_type=jnp.float32).astype(jnp.bfloat16)
    node_key = jnp.dot(node_norm, node_key_weight, preferred_element_type=jnp.float32).astype(jnp.bfloat16)
    node_value = jnp.dot(node_norm, node_value_weight, preferred_element_type=jnp.float32).astype(jnp.bfloat16)
    near_key = node_key[neighbour_index].reshape(CHAIN_LENGTH, K, NODE_HEADS, node_dim).astype(jnp.float32)
    near_value = node_value[neighbour_index].reshape(CHAIN_LENGTH, K, NODE_HEADS, node_dim).astype(jnp.float32)
    near_pos = coords[:, neighbour_index]
    offsets = near_pos - coords[:, :, None]
    dist2 = lax.optimization_barrier(jnp.sum(offsets * offsets, 0))
    queries = node_query.reshape(CHAIN_LENGTH, NODE_HEADS, node_dim).astype(jnp.float32)
    logits = jnp.einsum('ihd,ikhd->ihk', queries, near_key) * node_dim ** (-0.5)
    logits = logits - distance_penalty[None, :, None] * dist2[:, None, :]
    is_valid = jnp.arange(K, dtype=jnp.int32)[None, :] < neighbour_count[:, None]
    logits = jnp.where(is_valid[:, None, :], logits, -1e+30)
    node_weight = jax.nn.softmax(logits, axis=-1)
    node_weight = jnp.where(is_valid[:, None, :], node_weight, 0.0)
    weight_low = node_weight.astype(jnp.bfloat16).astype(jnp.float32)
    node_mix = jnp.einsum('ihk,ikhd->ihd', weight_low, near_value).reshape(CHAIN_LENGTH, C_NODE).astype(jnp.bfloat16)
    nodes_out = (nodes.astype(jnp.float32) + jnp.dot(node_mix, node_output_weight, preferred_element_type=jnp.float32)).astype(jnp.bfloat16)
    coord_pull = lax.optimization_barrier(jnp.sum(node_weight * coordinate_step[None, :, None], 1))
    coords_out = coords + lax.optimization_barrier(jnp.sum(offsets * coord_pull[None], -1))
    return (pair_out, nodes_out, coords_out)
```

```python
import functools

import jax
import jax.numpy as jnp
from jax import lax
from jax.experimental import pallas as pl
from jax.experimental.pallas import tpu as pltpu
from jax.sharding import PartitionSpec as P

PAIR_HEADS = 4
NODE_HEADS = 4
F32 = jnp.float32
BF16 = jnp.bfloat16
MESH = pl.DeviceIdType.MESH


def dot(a, b, ca=1, cb=0):
    return lax.dot_general(a, b, (((ca,), (cb,)), ((), ())), preferred_element_type=F32)


def normalize(x, gain):
    centred = x - jnp.mean(x, -1, keepdims=True)
    variance = jnp.mean(centred * centred, -1, keepdims=True)
    return centred * lax.rsqrt(variance + 1e-05) * gain


def row_to_column(row, size):
    across = lax.broadcasted_iota(jnp.int32, (size, size), 1)
    down = lax.broadcasted_iota(jnp.int32, (size, size), 0)
    return jnp.sum(jnp.where(across == down, row, 0.0), 1, keepdims=True)


def head_of_lane(shape, heads):
    return lax.broadcasted_iota(jnp.int32, shape, 1) // (shape[1] // heads)


def kernel(
    axes,
    msa_hbm, ids_hbm, lookup_hbm, msa_gain_hbm, w_left_hbm, w_right_hbm, w_outer_hbm, bias_hbm,
    pair_hbm, pair_gain_hbm, wq_hbm, wk_hbm, wv_hbm, wg_hbm, wo_hbm,
    nodes_hbm, coords_hbm, index_hbm, count_hbm, node_gain_hbm, nq_hbm, nk_hbm, nv_hbm, no_hbm,
    penalty_hbm, step_hbm,
    pair_out, nodes_out, coords_out,
    msa, ids, lookup, msa_gain, w_left, w_right, w_outer, bias, pair_gain, w_proj, wo,
    nodes, coords, index, count, node_gain, nw, no, penalty, step,
    pair_all, left_send, left_all, right_all, node_all, w_wide, w_flat, t_all, out_send,
    load_sem, send_sem, recv_sem, own_sem,
):
    n_seq, n_row, n_col = axes
    groups = n_seq * n_col
    seq, row, col = lax.axis_index("seq"), lax.axis_index("row"), lax.axis_index("col")
    g = seq * n_col + col
    seqs, rows_i, width_in = msa.shape
    product = w_left.shape[0]
    block = pair_all.shape[1]
    channels = wo.shape[0]
    rows_own = rows_i // groups
    cols = block // rows_own
    length = cols * groups
    total = seqs * groups

    def device(r, q):
        return (q // n_col, r, q % n_col)

    def others(position, size, body):
        def one(k, carry):
            body(lax.rem(position + k, size))
            return carry
        lax.fori_loop(1, size, one, 0, unroll=size <= 8)

    def group(body):
        others(g, groups, body)

    def rows_of_mesh(body):
        others(row, n_row, body)

    barrier = pltpu.get_barrier_semaphore()

    def greet(r, q):
        pl.semaphore_signal(barrier, inc=1, device_id=device(r, q), device_id_type=MESH)

    rows_of_mesh(lambda r: greet(r, g))
    group(lambda q: greet(row, q))

    def load(slot, source, target):
        copy = pltpu.make_async_copy(source, target, load_sem.at[slot])
        copy.start()
        return copy

    msa_loads = [
        load(0, ids_hbm, ids), load(1, msa_hbm, msa), load(2, lookup_hbm, lookup),
        load(3, msa_gain_hbm, msa_gain), load(4, w_left_hbm, w_left), load(5, w_right_hbm, w_right),
    ]
    node_loads = [load(6, nodes_hbm, nodes), load(7, coords_hbm, coords)]
    outer_loads = [load(8, w_outer_hbm, w_outer)]
    node_width = node_gain.shape[1]
    later_loads = [
        load(9, index_hbm, index), load(10, count_hbm, count), load(11, node_gain_hbm, node_gain),
        load(12, nq_hbm, nw.at[0]), load(13, nk_hbm, nw.at[1]), load(14, nv_hbm, nw.at[2]),
        load(15, no_hbm, no), load(16, penalty_hbm, penalty), load(17, step_hbm, step),
    ]
    pair_loads = [
        load(18, bias_hbm, bias), load(19, pair_gain_hbm, pair_gain),
        load(20, wq_hbm, w_proj.at[0]), load(21, wk_hbm, w_proj.at[1]),
        load(22, wv_hbm, w_proj.at[2]), load(23, wg_hbm, w_proj.at[3]), load(24, wo_hbm, wo),
    ]
    own_pair = pltpu.make_async_copy(pair_hbm.at[g], pair_all.at[g], own_sem.at[0])
    own_pair.start()

    for copy in msa_loads:
        copy.wait()
    kinds = lookup.shape[1]
    hot = []
    for s in range(seqs):
        column = row_to_column(ids[s : s + 1, :].astype(F32), rows_i).astype(jnp.int32)
        hot.append(column == lax.broadcasted_iota(jnp.int32, (rows_i, kinds), 1))
    hot = jnp.concatenate([h.astype(F32) for h in hot], 0).astype(BF16)
    embedded = dot(hot, lookup[...], 1, 1)
    msa_in = msa[...].astype(F32).reshape(seqs * rows_i, width_in) + embedded
    msa_norm = normalize(msa_in, msa_gain[...]).astype(BF16)
    left = dot(msa_norm, w_left[...], 1, 1).astype(BF16).astype(F32)
    right = dot(msa_norm, w_right[...], 1, 1)
    right_all[g * n_row + row] = jnp.concatenate(
        [right[s * rows_i : (s + 1) * rows_i] for s in range(seqs)], 1
    ).astype(BF16)
    for s in range(seqs):
        left_send[pl.ds(s, rows_i, stride=seqs), :] = left[s * rows_i : (s + 1) * rows_i]
    slab = rows_own * seqs
    left_all[g] = left_send[pl.ds(pl.multiple_of(g * slab, slab), slab), :]

    for copy in node_loads:
        copy.wait()
    local = nodes.shape[0]
    node_all[g] = jnp.concatenate(
        [nodes[...].astype(F32)]
        + [row_to_column(coords[x : x + 1, :], local) for x in range(3)]
        + [jnp.zeros((local, node_all.shape[2] - node_width - 3), F32)],
        1,
    )

    pl.semaphore_wait(barrier, n_row - 1 + groups - 1)

    def send(source, target, kind, r, q):
        pltpu.make_async_remote_copy(
            src_ref=source, dst_ref=target, send_sem=send_sem.at[kind], recv_sem=recv_sem.at[kind],
            device_id=device(r, q), device_id_type=MESH,
        ).start()

    mine = right_all.at[g * n_row + row]
    rows_of_mesh(lambda r: send(mine, mine, 5, r, g))
    group(lambda q: send(
        left_send.at[pl.ds(pl.multiple_of(q * slab, slab), slab)], left_all.at[g], 1, row, q
    ))
    group(lambda q: send(node_all.at[g], node_all.at[g], 3, row, q))
    group(lambda q: send(pair_hbm.at[q], pair_all.at[g], 2, row, q))

    def wait_bytes(ref, sem):
        pltpu.make_async_copy(ref, ref, sem).wait()

    for copy in outer_loads:
        copy.wait()
    w_flat[...] = w_outer[...].astype(F32)
    for d in range(product):
        w_wide[:, d * channels : (d + 1) * channels] = w_flat[
            pl.ds(d, product, stride=product), :
        ].astype(BF16)

    wait_bytes(right_all.at[pl.ds(0, n_row - 1)], recv_sem.at[5])
    gathered = right_all.at[pl.ds(g * n_row, n_row)]
    group(lambda q: send(gathered, gathered, 0, row, q))

    for copy in later_loads:
        copy.wait()
    slots = index.shape[1]
    counted = row_to_column(count[...].astype(F32), local)
    lane = lax.broadcasted_iota(jnp.int32, (local, slots), 1)
    live_index = jnp.where(lane.astype(F32) < counted, index[...], -1)
    everyone_n = lax.broadcasted_iota(jnp.int32, (local, length), 1)
    times = jnp.zeros((local, length), F32)
    for t in range(slots):
        times = times + jnp.where(live_index[:, t : t + 1] == everyone_n, 1.0, 0.0)
    wait_bytes(node_all.at[pl.ds(0, groups - 1)], recv_sem.at[3])
    table = node_all[...].reshape(length, node_all.shape[2])
    own = node_all[g]
    node_x = normalize(table[:, :node_width], node_gain[...]).astype(BF16)
    own_x = normalize(own[:, :node_width], node_gain[...]).astype(BF16)
    node_query = dot(own_x, nw[0])
    node_key = dot(node_x, nw[1]).astype(BF16)
    node_value = dot(node_x, nw[2]).astype(BF16)
    turned = table.T
    offsets = [
        turned[node_width + x : node_width + x + 1, :] - own[:, node_width + x : node_width + x + 1]
        for x in range(3)
    ]
    dist2 = offsets[0] * offsets[0] + offsets[1] * offsets[1] + offsets[2] * offsets[2]
    node_head = head_of_lane((local, node_width), NODE_HEADS)
    query_rows = jnp.concatenate(
        [jnp.where(node_head == h, node_query, 0.0) for h in range(NODE_HEADS)], 0
    ).astype(BF16)
    logits = dot(query_rows, node_key, 1, 1) * (node_width // NODE_HEADS) ** (-0.5)
    weighted = []
    pull = jnp.zeros((local, length), F32)
    for h in range(NODE_HEADS):
        rows = logits[h * local : (h + 1) * local] - penalty[:, h : h + 1] * dist2
        rows = jnp.where(times > 0.0, rows, -1e30)
        raised = times * jnp.exp(rows - jnp.max(rows, 1, keepdims=True))
        part = raised / jnp.sum(raised, 1, keepdims=True)
        weighted.append(part)
        pull = pull + step[:, h : h + 1] * part
    mixed = dot(jnp.concatenate(weighted, 0).astype(BF16), node_value)
    node_mix = jnp.zeros((local, node_width), F32)
    for h in range(NODE_HEADS):
        node_mix = jnp.where(node_head == h, mixed[h * local : (h + 1) * local], node_mix)
    nodes_out[...] = (nodes[...].astype(F32) + dot(node_mix.astype(BF16), no[...])).astype(BF16)
    down = lax.broadcasted_iota(jnp.int32, (local, local), 0)
    across = lax.broadcasted_iota(jnp.int32, (local, local), 1)
    moved = [
        jnp.sum(jnp.where(down == across, jnp.sum(offsets[x] * pull, 1, keepdims=True), 0.0), 0, keepdims=True)
        for x in range(3)
    ]
    coords_out[...] = coords[...] + jnp.concatenate(moved, 0)

    wait_bytes(left_all.at[pl.ds(0, groups - 1)], recv_sem.at[1])
    left_rows = left_all[...].reshape(groups * slab, product).astype(BF16)
    t_rows = dot(left_rows, w_wide[...]) * (1.0 / total)
    for d in range(product):
        t_all[pl.ds(d, groups * slab, stride=product), :] = t_rows[:, d * channels : (d + 1) * channels]
    deep = seqs * product
    t_pieces = [
        jnp.concatenate(
            [t_all[(q * rows_own + i) * deep : (q * rows_own + i + 1) * deep, :] for q in range(groups)], 0
        )
        for i in range(rows_own)
    ]
    t_joined = jnp.concatenate(t_pieces, 1).astype(BF16)
    own_pair.wait()
    wait_bytes(pair_all.at[pl.ds(0, groups - 1)], recv_sem.at[2])
    for copy in pair_loads:
        copy.wait()
    old = pair_all[...].astype(F32)
    wait_bytes(right_all.at[pl.ds(0, n_row * (groups - 1))], recv_sem.at[0])
    right_rows = jnp.concatenate(
        [right_all[q * n_row : (q + 1) * n_row].reshape(length, deep) for q in range(groups)], 1
    )
    update = dot(right_rows, t_joined)
    mid = jnp.concatenate(
        [
            jnp.concatenate([old[q, i * cols : (i + 1) * cols] for q in range(groups)], 0)
            + update[:, i * channels : (i + 1) * channels]
            for i in range(rows_own)
        ],
        0,
    )
    mid = (mid + bias[...]).astype(BF16).astype(F32)

    normed = normalize(mid, pair_gain[...]).astype(BF16)
    queries = dot(normed, w_proj[0])
    keys = dot(normed, w_proj[1]).astype(BF16)
    values = dot(normed, w_proj[2]).astype(BF16)
    gates = dot(normed, w_proj[3])
    head = head_of_lane((length, channels), PAIR_HEADS)
    scale = (channels // PAIR_HEADS) ** (-0.5)
    joined = []
    for i in range(rows_own):
        at = slice(i * length, (i + 1) * length)
        spread = jnp.concatenate(
            [jnp.where(head == h, queries[at], 0.0) for h in range(PAIR_HEADS)], 0
        ).astype(BF16)
        scores = dot(keys[at], spread, 1, 1) * scale
        raised = jnp.exp(scores - jnp.max(scores, 0, keepdims=True))
        weights = (raised * (1.0 / jnp.sum(raised, 0, keepdims=True))).astype(BF16)
        heads = dot(weights, values[at], 0, 0)
        taken = heads[:length]
        for h in range(1, PAIR_HEADS):
            taken = jnp.where(head == h, heads[h * length : (h + 1) * length], taken)
        joined.append(taken)
    attended = jnp.concatenate(joined, 0) * (1.0 / (1.0 + jnp.exp(-gates)))
    result = mid + dot(attended.astype(BF16), wo[...])
    for q in range(groups):
        out_send[q] = jnp.concatenate(
            [result[i * length + q * cols : i * length + (q + 1) * cols] for i in range(rows_own)], 0
        ).astype(BF16)

    group(lambda q: send(out_send.at[q], pair_out.at[g], 4, row, q))
    pair_out[g] = out_send[g]
    wait_bytes(right_all.at[pl.ds(0, n_row - 1)], send_sem.at[5])
    wait_bytes(right_all.at[pl.ds(0, n_row * (groups - 1))], send_sem.at[0])
    wait_bytes(left_all.at[pl.ds(0, groups - 1)], send_sem.at[1])
    wait_bytes(pair_all.at[pl.ds(0, groups - 1)], send_sem.at[2])
    wait_bytes(node_all.at[pl.ds(0, groups - 1)], send_sem.at[3])
    wait_bytes(out_send.at[pl.ds(0, groups - 1)], send_sem.at[4])
    wait_bytes(out_send.at[pl.ds(0, groups - 1)], recv_sem.at[4])


def hand_over(*refs):
    sources, targets, sem = refs[:3], refs[3:6], refs[6]
    copies = [pltpu.make_async_copy(a, b, sem.at[k]) for k, (a, b) in enumerate(zip(sources, targets))]
    for copy in copies:
        copy.start()
    for copy in copies:
        copy.wait()


def on_device(axes, *args):
    (msa, ids, lookup, msa_gain, w_left, w_right, w_outer, bias, pair, pair_gain, wq, wk, wv, wg, wo,
     nodes, coords, index, count, node_gain, nq, nk, nv, no, penalty, step) = args
    groups = axes[0] * axes[2]
    n = groups * axes[1]
    seqs, rows_i, width_in = msa.shape
    _, cols, channels = pair.shape
    rows_own = rows_i // groups
    block = rows_own * cols
    product = w_left.shape[1]
    lookup, w_left, w_right = lookup.T, w_left.T, w_right.T
    local, node_width = nodes.shape
    slab = rows_own * seqs
    as_row = lambda x: x.reshape(1, -1)
    vmem = lambda x: pltpu.VMEM(x.shape, x.dtype)
    msa_gain, bias, pair_gain, count, node_gain, penalty, step = map(
        as_row, (msa_gain, bias, pair_gain, count, node_gain, penalty, step)
    )
    pair = pair.reshape(groups, block, channels)
    operands = (msa, ids, lookup, msa_gain, w_left, w_right, w_outer, bias, pair, pair_gain, wq, wk, wv,
                wg, wo, nodes, coords, index, count, node_gain, nq, nk, nv, no, penalty, step)
    scratch = [vmem(x) for x in (msa, ids, lookup, msa_gain, w_left, w_right, w_outer, bias, pair_gain)]
    scratch += [pltpu.VMEM((4, channels, channels), BF16), vmem(wo)]
    scratch += [vmem(x) for x in (nodes, coords, index, count, node_gain)]
    scratch += [pltpu.VMEM((3, node_width, node_width), BF16), vmem(no), vmem(penalty), vmem(step)]
    scratch += [
        pltpu.VMEM((groups, block, channels), BF16),
        pltpu.VMEM((groups * slab, product), F32),
        pltpu.VMEM((groups, slab, product), F32),
        pltpu.VMEM((n, rows_i, seqs * product), BF16),
        pltpu.VMEM((groups, local, 128), F32),
        pltpu.VMEM((product, product * channels), BF16),
        pltpu.VMEM((product * product, channels), F32),
        pltpu.VMEM((groups * slab * product, channels), F32),
        pltpu.VMEM((groups, block, channels), BF16),
        pltpu.SemaphoreType.DMA((25,)),
        pltpu.SemaphoreType.DMA((6,)),
        pltpu.SemaphoreType.DMA((6,)),
        pltpu.SemaphoreType.DMA((1,)),
    ]
    hbm = pl.BlockSpec(memory_space=pl.ANY)
    results = pl.pallas_call(
        functools.partial(kernel, axes),
        out_shape=[
            pltpu.VMEM(pair.shape, BF16),
            pltpu.VMEM(nodes.shape, BF16),
            pltpu.VMEM(coords.shape, F32),
        ],
        in_specs=[hbm] * len(operands),
        out_specs=[pl.BlockSpec(memory_space=pltpu.VMEM)] * 3,
        scratch_shapes=scratch,
        compiler_params=pltpu.CompilerParams(
            collective_id=0, has_side_effects=True, vmem_limit_bytes=56 * 1024 * 1024
        ),
    )(*operands)
    pair_out, nodes_out, coords_out = pl.pallas_call(
        hand_over,
        out_shape=[jax.ShapeDtypeStruct(x.shape, x.dtype) for x in results],
        in_specs=[pl.BlockSpec(memory_space=pltpu.VMEM)] * 3,
        out_specs=[hbm] * 3,
        scratch_shapes=[pltpu.SemaphoreType.DMA((3,))],
    )(*results)
    return pair_out.reshape(rows_i, cols, channels), nodes_out, coords_out


def solution(mesh):
    axes = (mesh.shape["seq"], mesh.shape["row"], mesh.shape["col"])
    both = ("seq", "col")
    placed = (
        (P(both, "row", None), P(both, "row"))
        + (P(),) * 6
        + (P("row", both, None),)
        + (P(),) * 6
        + (P(both, None), P(None, both), P(both, None), P(both))
        + (P(),) * 7
    )
    return jax.shard_map(
        functools.partial(on_device, axes),
        mesh=mesh,
        in_specs=placed,
        out_specs=(P("row", both, None), P(both, None), P(None, both)),
        check_vma=False,
    )
```

```python
import functools

import jax
import jax.numpy as jnp
from jax import lax
from jax.experimental import pallas as pl
from jax.experimental.pallas import tpu as pltpu
from jax.sharding import PartitionSpec as P

PAIR_HEADS = 4
NODE_HEADS = 4
F32 = jnp.float32
BF16 = jnp.bfloat16
MESH = pl.DeviceIdType.MESH


def dot(a, b, ca=1, cb=0):
    return lax.dot_general(a, b, (((ca,), (cb,)), ((), ())), preferred_element_type=F32)


def normalize(x, gain):
    centred = x - jnp.mean(x, -1, keepdims=True)
    variance = jnp.mean(centred * centred, -1, keepdims=True)
    return centred * lax.rsqrt(variance + 1e-05) * gain


def row_to_column(row, size):
    across = lax.broadcasted_iota(jnp.int32, (size, size), 1)
    down = lax.broadcasted_iota(jnp.int32, (size, size), 0)
    return jnp.sum(jnp.where(across == down, row, 0.0), 1, keepdims=True)


def head_of_lane(shape, heads):
    return lax.broadcasted_iota(jnp.int32, shape, 1) // (shape[1] // heads)


def kernel(
    axes,
    msa_hbm, ids_hbm, lookup_hbm, msa_gain_hbm, w_left_hbm, w_right_hbm, w_outer_hbm, bias_hbm,
    pair_hbm, pair_gain_hbm, wq_hbm, wk_hbm, wv_hbm, wg_hbm, wo_hbm,
    nodes_hbm, coords_hbm, index_hbm, count_hbm, node_gain_hbm, nq_hbm, nk_hbm, nv_hbm, no_hbm,
    penalty_hbm, step_hbm,
    pair_out, nodes_out, coords_out,
    msa, ids, lookup, msa_gain, w_left, w_right, w_outer, bias, pair_gain, w_proj, wo,
    nodes, coords, index, count, node_gain, nw, no, penalty, step,
    pair_all, left_send, left_all, right_all, node_all, w_wide, w_flat, t_all, out_send,
    load_sem, send_sem, recv_sem, own_sem,
):
    n_seq, n_row, n_col = axes
    groups = n_seq * n_col
    seq, row, col = lax.axis_index("seq"), lax.axis_index("row"), lax.axis_index("col")
    g = seq * n_col + col
    seqs, rows_i, width_in = msa.shape
    product = w_left.shape[0]
    block = pair_all.shape[1]
    channels = wo.shape[0]
    rows_own = rows_i // groups
    cols = block // rows_own
    length = cols * groups
    total = seqs * groups

    def device(r, q):
        return (q // n_col, r, q % n_col)

    def others(position, size, body):
        def one(k, carry):
            body(lax.rem(position + k, size))
            return carry
        lax.fori_loop(1, size, one, 0, unroll=size <= 8)

    def group(body):
        others(g, groups, body)

    def rows_of_mesh(body):
        others(row, n_row, body)

    barrier = pltpu.get_barrier_semaphore()

    def greet(r, q):
        pl.semaphore_signal(barrier, inc=1, device_id=device(r, q), device_id_type=MESH)

    rows_of_mesh(lambda r: greet(r, g))
    group(lambda q: greet(row, q))

    def load(slot, source, target):
        copy = pltpu.make_async_copy(source, target, load_sem.at[slot])
        copy.start()
        return copy

    msa_loads = [
        load(0, ids_hbm, ids), load(1, msa_hbm, msa), load(2, lookup_hbm, lookup),
        load(3, msa_gain_hbm, msa_gain), load(4, w_left_hbm, w_left), load(5, w_right_hbm, w_right),
    ]
    node_loads = [load(6, nodes_hbm, nodes), load(7, coords_hbm, coords)]
    outer_loads = [load(8, w_outer_hbm, w_outer)]
    node_width = node_gain.shape[1]
    later_loads = [
        load(9, index_hbm, index), load(10, count_hbm, count), load(11, node_gain_hbm, node_gain),
        load(12, nq_hbm, nw.at[0]), load(13, nk_hbm, nw.at[1]), load(14, nv_hbm, nw.at[2]),
        load(15, no_hbm, no), load(16, penalty_hbm, penalty), load(17, step_hbm, step),
    ]
    pair_loads = [
        load(18, bias_hbm, bias), load(19, pair_gain_hbm, pair_gain),
        load(20, wq_hbm, w_proj.at[0]), load(21, wk_hbm, w_proj.at[1]),
        load(22, wv_hbm, w_proj.at[2]), load(23, wg_hbm, w_proj.at[3]), load(24, wo_hbm, wo),
    ]
    own_pair = pltpu.make_async_copy(pair_hbm.at[g], pair_all.at[g], own_sem.at[0])
    own_pair.start()

    for copy in msa_loads:
        copy.wait()
    kinds = lookup.shape[1]
    hot = []
    for s in range(seqs):
        column = row_to_column(ids[s : s + 1, :].astype(F32), rows_i).astype(jnp.int32)
        hot.append(column == lax.broadcasted_iota(jnp.int32, (rows_i, kinds), 1))
    hot = jnp.concatenate([h.astype(F32) for h in hot], 0).astype(BF16)
    embedded = dot(hot, lookup[...], 1, 1)
    msa_in = msa[...].astype(F32).reshape(seqs * rows_i, width_in) + embedded
    msa_norm = normalize(msa_in, msa_gain[...]).astype(BF16)
    left = dot(msa_norm, w_left[...], 1, 1).astype(BF16).astype(F32)
    right = dot(msa_norm, w_right[...], 1, 1)
    right_all[g * n_row + row] = jnp.concatenate(
        [right[s * rows_i : (s + 1) * rows_i] for s in range(seqs)], 1
    ).astype(BF16)
    for s in range(seqs):
        left_send[pl.ds(s, rows_i, stride=seqs), :] = left[s * rows_i : (s + 1) * rows_i]
    slab = rows_own * seqs
    left_all[g] = left_send[pl.ds(pl.multiple_of(g * slab, slab), slab), :]

    for copy in node_loads:
        copy.wait()
    local = nodes.shape[0]
    node_all[g] = jnp.concatenate(
        [nodes[...].astype(F32)]
        + [row_to_column(coords[x : x + 1, :], local) for x in range(3)]
        + [jnp.zeros((local, node_all.shape[2] - node_width - 3), F32)],
        1,
    )

    pl.semaphore_wait(barrier, n_row - 1 + groups - 1)

    def send(source, target, kind, r, q):
        pltpu.make_async_remote_copy(
            src_ref=source, dst_ref=target, send_sem=send_sem.at[kind], recv_sem=recv_sem.at[kind],
            device_id=device(r, q), device_id_type=MESH,
        ).start()

    mine = right_all.at[g * n_row + row]
    rows_of_mesh(lambda r: send(mine, mine, 5, r, g))
    group(lambda q: send(
        left_send.at[pl.ds(pl.multiple_of(q * slab, slab), slab)], left_all.at[g], 1, row, q
    ))
    group(lambda q: send(node_all.at[g], node_all.at[g], 3, row, q))
    group(lambda q: send(pair_hbm.at[q], pair_all.at[g], 2, row, q))

    def wait_bytes(ref, sem):
        pltpu.make_async_copy(ref, ref, sem).wait()

    for copy in outer_loads:
        copy.wait()
    w_flat[...] = w_outer[...].astype(F32)
    for d in range(product):
        w_wide[:, d * channels : (d + 1) * channels] = w_flat[
            pl.ds(d, product, stride=product), :
        ].astype(BF16)

    for copy in later_loads:
        copy.wait()
    slots = index.shape[1]
    counted = row_to_column(count[...].astype(F32), local)
    lane = lax.broadcasted_iota(jnp.int32, (local, slots), 1)
    live_index = jnp.where(lane.astype(F32) < counted, index[...], -1)
    everyone_n = lax.broadcasted_iota(jnp.int32, (local, length), 1)
    times = jnp.zeros((local, length), F32)
    for t in range(slots):
        times = times + jnp.where(live_index[:, t : t + 1] == everyone_n, 1.0, 0.0)

    wait_bytes(right_all.at[pl.ds(0, n_row - 1)], recv_sem.at[5])
    gathered = right_all.at[pl.ds(g * n_row, n_row)]
    group(lambda q: send(gathered, gathered, 0, row, q))

    wait_bytes(left_all.at[pl.ds(0, groups - 1)], recv_sem.at[1])
    left_rows = left_all[...].reshape(groups * slab, product).astype(BF16)
    t_rows = dot(left_rows, w_wide[...]) * (1.0 / total)
    for d in range(product):
        t_all[pl.ds(d, groups * slab, stride=product), :] = t_rows[:, d * channels : (d + 1) * channels]
    deep = seqs * product
    t_pieces = [
        jnp.concatenate(
            [t_all[(q * rows_own + i) * deep : (q * rows_own + i + 1) * deep, :] for q in range(groups)], 0
        )
        for i in range(rows_own)
    ]
    t_joined = jnp.concatenate(t_pieces, 1).astype(BF16)

    wait_bytes(node_all.at[pl.ds(0, groups - 1)], recv_sem.at[3])
    table = node_all[...].reshape(length, node_all.shape[2])
    own = node_all[g]
    node_x = normalize(table[:, :node_width], node_gain[...]).astype(BF16)
    own_x = normalize(own[:, :node_width], node_gain[...]).astype(BF16)
    node_query = dot(own_x, nw[0])
    node_key = dot(node_x, nw[1]).astype(BF16)
    node_value = dot(node_x, nw[2]).astype(BF16)
    turned = table.T
    offsets = [
        turned[node_width + x : node_width + x + 1, :] - own[:, node_width + x : node_width + x + 1]
        for x in range(3)
    ]
    dist2 = offsets[0] * offsets[0] + offsets[1] * offsets[1] + offsets[2] * offsets[2]
    own_pair.wait()
    wait_bytes(pair_all.at[pl.ds(0, groups - 1)], recv_sem.at[2])
    for copy in pair_loads:
        copy.wait()
    old = pair_all[...].astype(F32)
    wait_bytes(right_all.at[pl.ds(0, n_row * (groups - 1))], recv_sem.at[0])
    right_rows = jnp.concatenate(
        [right_all[q * n_row : (q + 1) * n_row].reshape(length, deep) for q in range(groups)], 1
    )
    update = dot(right_rows, t_joined)
    mid = jnp.concatenate(
        [
            jnp.concatenate([old[q, i * cols : (i + 1) * cols] for q in range(groups)], 0)
            + update[:, i * channels : (i + 1) * channels]
            for i in range(rows_own)
        ],
        0,
    )
    mid = (mid + bias[...]).astype(BF16).astype(F32)

    normed = normalize(mid, pair_gain[...]).astype(BF16)
    queries = dot(normed, w_proj[0])
    keys = dot(normed, w_proj[1]).astype(BF16)
    values = dot(normed, w_proj[2]).astype(BF16)
    gates = dot(normed, w_proj[3])
    head = head_of_lane((length, channels), PAIR_HEADS)
    scale = (channels // PAIR_HEADS) ** (-0.5)
    joined = []
    for i in range(rows_own):
        at = slice(i * length, (i + 1) * length)
        spread = jnp.concatenate(
            [jnp.where(head == h, queries[at], 0.0) for h in range(PAIR_HEADS)], 0
        ).astype(BF16)
        scores = dot(keys[at], spread, 1, 1) * scale
        raised = jnp.exp(scores - jnp.max(scores, 0, keepdims=True))
        weights = (raised * (1.0 / jnp.sum(raised, 0, keepdims=True))).astype(BF16)
        heads = dot(weights, values[at], 0, 0)
        taken = heads[:length]
        for h in range(1, PAIR_HEADS):
            taken = jnp.where(head == h, heads[h * length : (h + 1) * length], taken)
        joined.append(taken)
    attended = jnp.concatenate(joined, 0) * (1.0 / (1.0 + jnp.exp(-gates)))
    result = mid + dot(attended.astype(BF16), wo[...])
    for q in range(groups):
        out_send[q] = jnp.concatenate(
            [result[i * length + q * cols : i * length + (q + 1) * cols] for i in range(rows_own)], 0
        ).astype(BF16)

    group(lambda q: send(out_send.at[q], pair_out.at[g], 4, row, q))
    pair_out[g] = out_send[g]
    node_head = head_of_lane((local, node_width), NODE_HEADS)
    query_rows = jnp.concatenate(
        [jnp.where(node_head == h, node_query, 0.0) for h in range(NODE_HEADS)], 0
    ).astype(BF16)
    logits = dot(query_rows, node_key, 1, 1) * (node_width // NODE_HEADS) ** (-0.5)
    weighted = []
    pull = jnp.zeros((local, length), F32)
    for h in range(NODE_HEADS):
        rows = logits[h * local : (h + 1) * local] - penalty[:, h : h + 1] * dist2
        rows = jnp.where(times > 0.0, rows, -1e30)
        raised = times * jnp.exp(rows - jnp.max(rows, 1, keepdims=True))
        part = raised / jnp.sum(raised, 1, keepdims=True)
        weighted.append(part)
        pull = pull + step[:, h : h + 1] * part
    mixed = dot(jnp.concatenate(weighted, 0).astype(BF16), node_value)
    node_mix = jnp.zeros((local, node_width), F32)
    for h in range(NODE_HEADS):
        node_mix = jnp.where(node_head == h, mixed[h * local : (h + 1) * local], node_mix)
    nodes_out[...] = (nodes[...].astype(F32) + dot(node_mix.astype(BF16), no[...])).astype(BF16)
    down = lax.broadcasted_iota(jnp.int32, (local, local), 0)
    across = lax.broadcasted_iota(jnp.int32, (local, local), 1)
    moved = [
        jnp.sum(jnp.where(down == across, jnp.sum(offsets[x] * pull, 1, keepdims=True), 0.0), 0, keepdims=True)
        for x in range(3)
    ]
    coords_out[...] = coords[...] + jnp.concatenate(moved, 0)

    wait_bytes(right_all.at[pl.ds(0, n_row - 1)], send_sem.at[5])
    wait_bytes(right_all.at[pl.ds(0, n_row * (groups - 1))], send_sem.at[0])
    wait_bytes(left_all.at[pl.ds(0, groups - 1)], send_sem.at[1])
    wait_bytes(pair_all.at[pl.ds(0, groups - 1)], send_sem.at[2])
    wait_bytes(node_all.at[pl.ds(0, groups - 1)], send_sem.at[3])
    wait_bytes(out_send.at[pl.ds(0, groups - 1)], send_sem.at[4])
    wait_bytes(out_send.at[pl.ds(0, groups - 1)], recv_sem.at[4])


def hand_over(*refs):
    sources, targets, sem = refs[:3], refs[3:6], refs[6]
    copies = [pltpu.make_async_copy(a, b, sem.at[k]) for k, (a, b) in enumerate(zip(sources, targets))]
    for copy in copies:
        copy.start()
    for copy in copies:
        copy.wait()


def on_device(axes, *args):
    (msa, ids, lookup, msa_gain, w_left, w_right, w_outer, bias, pair, pair_gain, wq, wk, wv, wg, wo,
     nodes, coords, index, count, node_gain, nq, nk, nv, no, penalty, step) = args
    groups = axes[0] * axes[2]
    n = groups * axes[1]
    seqs, rows_i, width_in = msa.shape
    _, cols, channels = pair.shape
    rows_own = rows_i // groups
    block = rows_own * cols
    product = w_left.shape[1]
    lookup, w_left, w_right = lookup.T, w_left.T, w_right.T
    local, node_width = nodes.shape
    slab = rows_own * seqs
    as_row = lambda x: x.reshape(1, -1)
    vmem = lambda x: pltpu.VMEM(x.shape, x.dtype)
    msa_gain, bias, pair_gain, count, node_gain, penalty, step = map(
        as_row, (msa_gain, bias, pair_gain, count, node_gain, penalty, step)
    )
    pair = pair.reshape(groups, block, channels)
    operands = (msa, ids, lookup, msa_gain, w_left, w_right, w_outer, bias, pair, pair_gain, wq, wk, wv,
                wg, wo, nodes, coords, index, count, node_gain, nq, nk, nv, no, penalty, step)
    scratch = [vmem(x) for x in (msa, ids, lookup, msa_gain, w_left, w_right, w_outer, bias, pair_gain)]
    scratch += [pltpu.VMEM((4, channels, channels), BF16), vmem(wo)]
    scratch += [vmem(x) for x in (nodes, coords, index, count, node_gain)]
    scratch += [pltpu.VMEM((3, node_width, node_width), BF16), vmem(no), vmem(penalty), vmem(step)]
    scratch += [
        pltpu.VMEM((groups, block, channels), BF16),
        pltpu.VMEM((groups * slab, product), F32),
        pltpu.VMEM((groups, slab, product), F32),
        pltpu.VMEM((n, rows_i, seqs * product), BF16),
        pltpu.VMEM((groups, local, 128), F32),
        pltpu.VMEM((product, product * channels), BF16),
        pltpu.VMEM((product * product, channels), F32),
        pltpu.VMEM((groups * slab * product, channels), F32),
        pltpu.VMEM((groups, block, channels), BF16),
        pltpu.SemaphoreType.DMA((25,)),
        pltpu.SemaphoreType.DMA((6,)),
        pltpu.SemaphoreType.DMA((6,)),
        pltpu.SemaphoreType.DMA((1,)),
    ]
    hbm = pl.BlockSpec(memory_space=pl.ANY)
    results = pl.pallas_call(
        functools.partial(kernel, axes),
        out_shape=[
            pltpu.VMEM(pair.shape, BF16),
            pltpu.VMEM(nodes.shape, BF16),
            pltpu.VMEM(coords.shape, F32),
        ],
        in_specs=[hbm] * len(operands),
        out_specs=[pl.BlockSpec(memory_space=pltpu.VMEM)] * 3,
        scratch_shapes=scratch,
        compiler_params=pltpu.CompilerParams(
            collective_id=0, has_side_effects=True, vmem_limit_bytes=56 * 1024 * 1024
        ),
    )(*operands)
    pair_out, nodes_out, coords_out = pl.pallas_call(
        hand_over,
        out_shape=[jax.ShapeDtypeStruct(x.shape, x.dtype) for x in results],
        in_specs=[pl.BlockSpec(memory_space=pltpu.VMEM)] * 3,
        out_specs=[hbm] * 3,
        scratch_shapes=[pltpu.SemaphoreType.DMA((3,))],
        compiler_params=pltpu.CompilerParams(vmem_limit_bytes=1024 * 1024),
    )(*results)
    return pair_out.reshape(rows_i, cols, channels), nodes_out, coords_out


def solution(mesh):
    axes = (mesh.shape["seq"], mesh.shape["row"], mesh.shape["col"])
    both = ("seq", "col")
    placed = (
        (P(both, "row", None), P(both, "row"))
        + (P(),) * 6
        + (P("row", both, None),)
        + (P(),) * 6
        + (P(both, None), P(None, both), P(both, None), P(both))
        + (P(),) * 7
    )
    return jax.shard_map(
        functools.partial(on_device, axes),
        mesh=mesh,
        in_specs=placed,
        out_specs=(P("row", both, None), P(both, None), P(None, both)),
        check_vma=False,
    )
```

```python
import functools

import jax
import jax.numpy as jnp
from jax import lax
from jax.experimental import pallas as pl
from jax.experimental.pallas import tpu as pltpu
from jax.sharding import PartitionSpec as P

PAIR_HEADS = 4
NODE_HEADS = 4
F32 = jnp.float32
BF16 = jnp.bfloat16
MESH = pl.DeviceIdType.MESH


def dot(a, b, ca=1, cb=0):
    return lax.dot_general(a, b, (((ca,), (cb,)), ((), ())), preferred_element_type=F32)


def normalize(x, gain):
    centred = x - jnp.mean(x, -1, keepdims=True)
    variance = jnp.mean(centred * centred, -1, keepdims=True)
    return centred * lax.rsqrt(variance + 1e-05) * gain


def row_to_column(row, size):
    across = lax.broadcasted_iota(jnp.int32, (size, size), 1)
    down = lax.broadcasted_iota(jnp.int32, (size, size), 0)
    return jnp.sum(jnp.where(across == down, row, 0.0), 1, keepdims=True)


def head_of_lane(shape, heads):
    return lax.broadcasted_iota(jnp.int32, shape, 1) // (shape[1] // heads)


def kernel(
    axes,
    msa_hbm, ids_hbm, lookup_hbm, msa_gain_hbm, w_left_hbm, w_right_hbm, w_outer_hbm, bias_hbm,
    pair_hbm, pair_gain_hbm, wq_hbm, wk_hbm, wv_hbm, wg_hbm, wo_hbm,
    nodes_hbm, coords_hbm, index_hbm, count_hbm, node_gain_hbm, nq_hbm, nk_hbm, nv_hbm, no_hbm,
    penalty_hbm, step_hbm,
    pair_out, nodes_out, coords_out,
    msa, ids, lookup, msa_gain, w_left, w_right, w_outer, bias, pair_gain, w_proj, wo,
    nodes, coords, index, count, node_gain, nw, no, penalty, step,
    pair_all, left_send, left_all, right_all, node_all, w_wide, w_flat, t_all, out_send,
    load_sem, send_sem, recv_sem, own_sem,
):
    n_seq, n_row, n_col = axes
    groups = n_seq * n_col
    seq, row, col = lax.axis_index("seq"), lax.axis_index("row"), lax.axis_index("col")
    g = seq * n_col + col
    seqs, rows_i, width_in = msa.shape
    product = w_left.shape[0]
    block = pair_all.shape[1]
    channels = wo.shape[0]
    rows_own = rows_i // groups
    cols = block // rows_own
    length = cols * groups
    total = seqs * groups

    def device(r, q):
        return (q // n_col, r, q % n_col)

    def others(position, size, body):
        def one(k, carry):
            body(lax.rem(position + k, size))
            return carry
        lax.fori_loop(1, size, one, 0, unroll=size <= 8)

    def group(body):
        others(g, groups, body)

    toward = jnp.where(2 * row < n_row, 1, n_row - 1)

    def rows_of_mesh(body, far_first=False):
        for k in range(1, n_row):
            body(lax.rem(row + (n_row - k if far_first else k) * toward, n_row))

    barrier = pltpu.get_barrier_semaphore()

    def greet(r, q):
        pl.semaphore_signal(barrier, inc=1, device_id=device(r, q), device_id_type=MESH)

    def load(slot, source, target):
        copy = pltpu.make_async_copy(source, target, load_sem.at[slot])
        copy.start()
        return copy

    msa_loads = [
        load(0, ids_hbm, ids), load(1, msa_hbm, msa), load(2, lookup_hbm, lookup),
        load(3, msa_gain_hbm, msa_gain), load(4, w_left_hbm, w_left), load(5, w_right_hbm, w_right),
    ]
    rows_of_mesh(lambda r: greet(r, g))
    group(lambda q: greet(row, q))
    node_loads = [load(6, nodes_hbm, nodes), load(7, coords_hbm, coords)]
    outer_loads = [load(8, w_outer_hbm, w_outer)]
    node_width = node_gain.shape[1]
    later_loads = [
        load(9, index_hbm, index), load(10, count_hbm, count), load(11, node_gain_hbm, node_gain),
        load(12, nq_hbm, nw.at[0]), load(13, nk_hbm, nw.at[1]), load(14, nv_hbm, nw.at[2]),
        load(15, no_hbm, no), load(16, penalty_hbm, penalty), load(17, step_hbm, step),
    ]
    pair_loads = [
        load(18, bias_hbm, bias), load(19, pair_gain_hbm, pair_gain),
        load(20, wq_hbm, w_proj.at[0]), load(21, wk_hbm, w_proj.at[1]),
        load(22, wv_hbm, w_proj.at[2]), load(23, wg_hbm, w_proj.at[3]), load(24, wo_hbm, wo),
    ]
    own_pair = pltpu.make_async_copy(pair_hbm.at[g], pair_all.at[g], own_sem.at[0])
    own_pair.start()

    for copy in msa_loads:
        copy.wait()
    kinds = lookup.shape[1]
    hot = []
    for s in range(seqs):
        column = row_to_column(ids[s : s + 1, :].astype(F32), rows_i).astype(jnp.int32)
        hot.append(column == lax.broadcasted_iota(jnp.int32, (rows_i, kinds), 1))
    hot = jnp.concatenate([h.astype(F32) for h in hot], 0).astype(BF16)
    embedded = dot(hot, lookup[...], 1, 1)
    msa_in = msa[...].astype(F32).reshape(seqs * rows_i, width_in) + embedded
    msa_norm = normalize(msa_in, msa_gain[...]).astype(BF16)
    left = dot(msa_norm, w_left[...], 1, 1).astype(BF16).astype(F32)
    right = dot(msa_norm, w_right[...], 1, 1)
    right_all[g * n_row + row] = jnp.concatenate(
        [right[s * rows_i : (s + 1) * rows_i] for s in range(seqs)], 1
    ).astype(BF16)
    for s in range(seqs):
        left_send[pl.ds(s, rows_i, stride=seqs), :] = left[s * rows_i : (s + 1) * rows_i]
    slab = rows_own * seqs
    left_all[g] = left_send[pl.ds(pl.multiple_of(g * slab, slab), slab), :]

    for copy in node_loads:
        copy.wait()
    local = nodes.shape[0]
    node_all[g] = jnp.concatenate(
        [nodes[...].astype(F32)]
        + [row_to_column(coords[x : x + 1, :], local) for x in range(3)]
        + [jnp.zeros((local, node_all.shape[2] - node_width - 3), F32)],
        1,
    )

    pl.semaphore_wait(barrier, n_row - 1 + groups - 1)

    def send(source, target, kind, r, q, arrival=None):
        pltpu.make_async_remote_copy(
            src_ref=source, dst_ref=target, send_sem=send_sem.at[kind],
            recv_sem=recv_sem.at[kind if arrival is None else arrival],
            device_id=device(r, q), device_id_type=MESH,
        ).start()

    mine = right_all.at[g * n_row + row]
    rows_of_mesh(lambda r: send(mine, mine, 5, r, g, 5 + row), far_first=True)
    group(lambda q: send(mine, mine, 0, row, q))
    group(lambda q: send(
        left_send.at[pl.ds(pl.multiple_of(q * slab, slab), slab)], left_all.at[g], 1, row, q
    ))
    group(lambda q: send(node_all.at[g], node_all.at[g], 3, row, q))
    group(lambda q: send(pair_hbm.at[q], pair_all.at[g], 2, row, q))

    def wait_bytes(ref, sem):
        pltpu.make_async_copy(ref, ref, sem).wait()

    for copy in outer_loads:
        copy.wait()
    w_flat[...] = w_outer[...].astype(F32)
    for d in range(product):
        w_wide[:, d * channels : (d + 1) * channels] = w_flat[
            pl.ds(d, product, stride=product), :
        ].astype(BF16)

    def forward(r):
        arrived = right_all.at[g * n_row + r]
        wait_bytes(arrived, recv_sem.at[5 + r])
        group(lambda q: send(arrived, arrived, 0, row, q))

    rows_of_mesh(forward)

    wait_bytes(left_all.at[pl.ds(0, groups - 1)], recv_sem.at[1])
    left_rows = left_all[...].reshape(groups * slab, product).astype(BF16)
    t_rows = dot(left_rows, w_wide[...]) * (1.0 / total)
    for d in range(product):
        t_all[pl.ds(d, groups * slab, stride=product), :] = t_rows[:, d * channels : (d + 1) * channels]
    deep = seqs * product
    t_pieces = [
        jnp.concatenate(
            [t_all[(q * rows_own + i) * deep : (q * rows_own + i + 1) * deep, :] for q in range(groups)], 0
        )
        for i in range(rows_own)
    ]
    t_joined = jnp.concatenate(t_pieces, 1).astype(BF16)

    for copy in later_loads:
        copy.wait()
    slots = index.shape[1]
    counted = row_to_column(count[...].astype(F32), local)
    lane = lax.broadcasted_iota(jnp.int32, (local, slots), 1)
    live_index = jnp.where(lane.astype(F32) < counted, index[...], -1)
    everyone_n = lax.broadcasted_iota(jnp.int32, (local, length), 1)
    times = jnp.zeros((local, length), F32)
    for t in range(slots):
        times = times + jnp.where(live_index[:, t : t + 1] == everyone_n, 1.0, 0.0)

    wait_bytes(node_all.at[pl.ds(0, groups - 1)], recv_sem.at[3])
    table = node_all[...].reshape(length, node_all.shape[2])
    own = node_all[g]
    node_x = normalize(table[:, :node_width], node_gain[...]).astype(BF16)
    own_x = normalize(own[:, :node_width], node_gain[...]).astype(BF16)
    node_query = dot(own_x, nw[0])
    node_key = dot(node_x, nw[1]).astype(BF16)
    node_value = dot(node_x, nw[2]).astype(BF16)
    turned = table.T
    offsets = [
        turned[node_width + x : node_width + x + 1, :] - own[:, node_width + x : node_width + x + 1]
        for x in range(3)
    ]
    dist2 = offsets[0] * offsets[0] + offsets[1] * offsets[1] + offsets[2] * offsets[2]
    own_pair.wait()
    wait_bytes(pair_all.at[pl.ds(0, groups - 1)], recv_sem.at[2])
    for copy in pair_loads:
        copy.wait()
    old = pair_all[...].astype(F32)
    wait_bytes(right_all.at[pl.ds(0, n_row * (groups - 1))], recv_sem.at[0])
    right_rows = jnp.concatenate(
        [right_all[q * n_row : (q + 1) * n_row].reshape(length, deep) for q in range(groups)], 1
    )
    update = dot(right_rows, t_joined)
    mid = jnp.concatenate(
        [
            jnp.concatenate([old[q, i * cols : (i + 1) * cols] for q in range(groups)], 0)
            + update[:, i * channels : (i + 1) * channels]
            for i in range(rows_own)
        ],
        0,
    )
    mid = (mid + bias[...]).astype(BF16).astype(F32)

    normed = normalize(mid, pair_gain[...]).astype(BF16)
    queries = dot(normed, w_proj[0])
    keys = dot(normed, w_proj[1]).astype(BF16)
    values = dot(normed, w_proj[2]).astype(BF16)
    gates = dot(normed, w_proj[3])
    head = head_of_lane((length, channels), PAIR_HEADS)
    scale = (channels // PAIR_HEADS) ** (-0.5)
    joined = []
    for i in range(rows_own):
        at = slice(i * length, (i + 1) * length)
        spread = jnp.concatenate(
            [jnp.where(head == h, queries[at], 0.0) for h in range(PAIR_HEADS)], 0
        ).astype(BF16)
        scores = dot(keys[at], spread, 1, 1) * scale
        raised = jnp.exp(scores - jnp.max(scores, 0, keepdims=True))
        weights = (raised * (1.0 / jnp.sum(raised, 0, keepdims=True))).astype(BF16)
        heads = dot(weights, values[at], 0, 0)
        taken = heads[:length]
        for h in range(1, PAIR_HEADS):
            taken = jnp.where(head == h, heads[h * length : (h + 1) * length], taken)
        joined.append(taken)
    attended = jnp.concatenate(joined, 0) * (1.0 / (1.0 + jnp.exp(-gates)))
    result = mid + dot(attended.astype(BF16), wo[...])
    for q in range(groups):
        out_send[q] = jnp.concatenate(
            [result[i * length + q * cols : i * length + (q + 1) * cols] for i in range(rows_own)], 0
        ).astype(BF16)

    group(lambda q: send(out_send.at[q], pair_out.at[g], 4, row, q))
    pair_out[g] = out_send[g]
    node_head = head_of_lane((local, node_width), NODE_HEADS)
    query_rows = jnp.concatenate(
        [jnp.where(node_head == h, node_query, 0.0) for h in range(NODE_HEADS)], 0
    ).astype(BF16)
    logits = dot(query_rows, node_key, 1, 1) * (node_width // NODE_HEADS) ** (-0.5)
    weighted = []
    pull = jnp.zeros((local, length), F32)
    for h in range(NODE_HEADS):
        rows = logits[h * local : (h + 1) * local] - penalty[:, h : h + 1] * dist2
        rows = jnp.where(times > 0.0, rows, -1e30)
        raised = times * jnp.exp(rows - jnp.max(rows, 1, keepdims=True))
        part = raised / jnp.sum(raised, 1, keepdims=True)
        weighted.append(part)
        pull = pull + step[:, h : h + 1] * part
    mixed = dot(jnp.concatenate(weighted, 0).astype(BF16), node_value)
    node_mix = jnp.zeros((local, node_width), F32)
    for h in range(NODE_HEADS):
        node_mix = jnp.where(node_head == h, mixed[h * local : (h + 1) * local], node_mix)
    nodes_out[...] = (nodes[...].astype(F32) + dot(node_mix.astype(BF16), no[...])).astype(BF16)
    down = lax.broadcasted_iota(jnp.int32, (local, local), 0)
    across = lax.broadcasted_iota(jnp.int32, (local, local), 1)
    moved = [
        jnp.sum(jnp.where(down == across, jnp.sum(offsets[x] * pull, 1, keepdims=True), 0.0), 0, keepdims=True)
        for x in range(3)
    ]
    coords_out[...] = coords[...] + jnp.concatenate(moved, 0)

    wait_bytes(right_all.at[pl.ds(0, n_row - 1)], send_sem.at[5])
    wait_bytes(right_all.at[pl.ds(0, n_row * (groups - 1))], send_sem.at[0])
    wait_bytes(left_all.at[pl.ds(0, groups - 1)], send_sem.at[1])
    wait_bytes(pair_all.at[pl.ds(0, groups - 1)], send_sem.at[2])
    wait_bytes(node_all.at[pl.ds(0, groups - 1)], send_sem.at[3])
    wait_bytes(out_send.at[pl.ds(0, groups - 1)], send_sem.at[4])
    wait_bytes(out_send.at[pl.ds(0, groups - 1)], recv_sem.at[4])


def hand_over(*refs):
    sources, targets, sem = refs[:3], refs[3:6], refs[6]
    copies = [pltpu.make_async_copy(a, b, sem.at[k]) for k, (a, b) in enumerate(zip(sources, targets))]
    for copy in copies:
        copy.start()
    for copy in copies:
        copy.wait()


def on_device(axes, *args):
    (msa, ids, lookup, msa_gain, w_left, w_right, w_outer, bias, pair, pair_gain, wq, wk, wv, wg, wo,
     nodes, coords, index, count, node_gain, nq, nk, nv, no, penalty, step) = args
    groups = axes[0] * axes[2]
    n = groups * axes[1]
    seqs, rows_i, width_in = msa.shape
    _, cols, channels = pair.shape
    rows_own = rows_i // groups
    block = rows_own * cols
    product = w_left.shape[1]
    lookup, w_left, w_right = lookup.T, w_left.T, w_right.T
    local, node_width = nodes.shape
    slab = rows_own * seqs
    as_row = lambda x: x.reshape(1, -1)
    vmem = lambda x: pltpu.VMEM(x.shape, x.dtype)
    msa_gain, bias, pair_gain, count, node_gain, penalty, step = map(
        as_row, (msa_gain, bias, pair_gain, count, node_gain, penalty, step)
    )
    pair = pair.reshape(groups, block, channels)
    operands = (msa, ids, lookup, msa_gain, w_left, w_right, w_outer, bias, pair, pair_gain, wq, wk, wv,
                wg, wo, nodes, coords, index, count, node_gain, nq, nk, nv, no, penalty, step)
    scratch = [vmem(x) for x in (msa, ids, lookup, msa_gain, w_left, w_right, w_outer, bias, pair_gain)]
    scratch += [pltpu.VMEM((4, channels, channels), BF16), vmem(wo)]
    scratch += [vmem(x) for x in (nodes, coords, index, count, node_gain)]
    scratch += [pltpu.VMEM((3, node_width, node_width), BF16), vmem(no), vmem(penalty), vmem(step)]
    scratch += [
        pltpu.VMEM((groups, block, channels), BF16),
        pltpu.VMEM((groups * slab, product), F32),
        pltpu.VMEM((groups, slab, product), F32),
        pltpu.VMEM((n, rows_i, seqs * product), BF16),
        pltpu.VMEM((groups, local, 128), F32),
        pltpu.VMEM((product, product * channels), BF16),
        pltpu.VMEM((product * product, channels), F32),
        pltpu.VMEM((groups * slab * product, channels), F32),
        pltpu.VMEM((groups, block, channels), BF16),
        pltpu.SemaphoreType.DMA((25,)),
        pltpu.SemaphoreType.DMA((6,)),
        pltpu.SemaphoreType.DMA((5 + axes[1],)),
        pltpu.SemaphoreType.DMA((1,)),
    ]
    hbm = pl.BlockSpec(memory_space=pl.ANY)
    results = pl.pallas_call(
        functools.partial(kernel, axes),
        out_shape=[
            pltpu.VMEM(pair.shape, BF16),
            pltpu.VMEM(nodes.shape, BF16),
            pltpu.VMEM(coords.shape, F32),
        ],
        in_specs=[hbm] * len(operands),
        out_specs=[pl.BlockSpec(memory_space=pltpu.VMEM)] * 3,
        scratch_shapes=scratch,
        compiler_params=pltpu.CompilerParams(
            collective_id=0, has_side_effects=True, vmem_limit_bytes=56 * 1024 * 1024
        ),
    )(*operands)
    pair_out, nodes_out, coords_out = pl.pallas_call(
        hand_over,
        out_shape=[jax.ShapeDtypeStruct(x.shape, x.dtype) for x in results],
        in_specs=[pl.BlockSpec(memory_space=pltpu.VMEM)] * 3,
        out_specs=[hbm] * 3,
        scratch_shapes=[pltpu.SemaphoreType.DMA((3,))],
        compiler_params=pltpu.CompilerParams(vmem_limit_bytes=1024 * 1024),
    )(*results)
    return pair_out.reshape(rows_i, cols, channels), nodes_out, coords_out


def solution(mesh):
    axes = (mesh.shape["seq"], mesh.shape["row"], mesh.shape["col"])
    both = ("seq", "col")
    placed = (
        (P(both, "row", None), P(both, "row"))
        + (P(),) * 6
        + (P("row", both, None),)
        + (P(),) * 6
        + (P(both, None), P(None, both), P(both, None), P(both))
        + (P(),) * 7
    )
    return jax.shard_map(
        functools.partial(on_device, axes),
        mesh=mesh,
        in_specs=placed,
        out_specs=(P("row", both, None), P(both, None), P(None, both)),
        check_vma=False,
    )
```
